128 devices in a mesh: row: 16 (over x, y), col: 4 (over z), depth: 2 (over core).
Axes of the slice: x: 4, y: 4, z: 4, core: 2. Of those that a mesh axis runs over, the one named last changes fastest.
Arguments:
- p_blocks: float32 [160, 4, 6, 128, 128], P('row', 'col', 'depth'), may hold values from -0.125 to 0.125
- s_blocks: float32 [160, 4, 6, 128, 128], P('row', 'col'), may hold values from -6 to 6
- p_pattern: int32 [160, 4, 6], P('row'), may hold values from -1 to 159, as said below
- s_pattern: int32 [160, 4, 6], P(None, 'col'), may hold values from -1 to 159, as said below
Outputs:
- product: float32 [160, 4, 6, 128, 128], P('row', 'col', 'depth')
The draws below stay inside these ranges and needn't reach their ends.
Inputs may be any that keep to these rules, and one draw needn't show every extreme that they name: `p_pattern`: in each row and group of slots the filled slots come first. Every block column belongs to one grid column, the same in both patterns, and appears only in that group of slots; the columns of a block row are distinct and lie within cyclic distance 10 of the row, modulo 160. Some block row fills all 6 slots of some group. `s_pattern`: as for p_pattern, with the same grid column for each block column.
All inputs are finite; a program needn't handle non-finite values.
Results may differ from the reference program's by a relative error of at most 0.0003.
Values sent between devices are 32-bit elements; how exact they have to be, the bound alone decides.
A program may use at most 128 MiB of HBM per device.

```python
import jax
import jax.numpy as jnp
from jax import lax

BS = 128
W = 10
NB = 160
KT = 6
N_COL = 4


def owner_table(key):
    run_count = NB // N_COL
    key_list = jax.random.split(jax.random.fold_in(key, 7), run_count)
    shuffles = jax.vmap(lambda sub_key: jax.random.permutation(sub_key, N_COL))(key_list)
    return shuffles.reshape(NB).astype(jnp.int32)


def pattern(key, stream_id):
    owners = owner_table(key)
    offsets = jnp.arange(2 * W + 1, dtype=jnp.int32) - W
    row_ids = jnp.arange(NB, dtype=jnp.int32)
    column_ids = (row_ids[:, None] + offsets[None, :]) % NB
    coin_toss = jax.random.randint(jax.random.fold_in(key, stream_id), (NB, 2 * W + 1), 0, 4)
    full_rows = jax.random.randint(jax.random.fold_in(key, stream_id + 100), (NB,), 0, 4)
    whole_row = (full_rows == 0) | (row_ids == 0)
    kept_mask = (coin_toss != 0) | whole_row[:, None] | (offsets[None, :] == 0)
    group_ids = owners[column_ids]
    member = kept_mask[:, None, :] & (group_ids[:, None, :] == jnp.arange(N_COL, dtype=jnp.int32)[None, :, None])
    position = jnp.cumsum(member.astype(jnp.int32), axis=2) - 1
    slot_hit = member[..., None] & (position[..., None] == jnp.arange(KT, dtype=jnp.int32)[None, None, None, :])
    filled = jnp.any(slot_hit, axis=2)
    picked = jnp.sum(jnp.where(slot_hit, column_ids[:, None, :, None], 0), axis=2)
    return jnp.where(filled, picked, -1).astype(jnp.int32)


def draw_p_pattern(key, part):
    return pattern(key, 1)


def draw_s_pattern(key, part):
    return pattern(key, 2)


def level_of(stream_key, dims, cuts, low, top_value):
    def one(axis_at, parts):
        steps = jax.random.uniform(jax.random.fold_in(jax.random.fold_in(stream_key, 6), axis_at), (parts,), jnp.float32, low / len(cuts), top_value / len(cuts))
        return jnp.repeat(jnp.exp(steps), dims[axis_at] // parts).reshape((-1,) + (1,) * (len(dims) - axis_at - 1))

    level = one(*cuts[0])
    for cut in cuts[1:]:
        level = level * one(*cut)
    return level


def bell_draw(rng, shape, spread, limit, cuts=(), kind=jnp.bfloat16):
    result = spread * jax.random.normal(rng, shape, jnp.float32)
    if cuts:
        result = result * level_of(rng, shape, cuts, -0.22, 0.18)
    return jnp.clip(result, -limit, limit).astype(kind)


def setup_inputs(seed: int = 0) -> dict:
    seeds = jax.random.split(jax.random.key(seed), 5)
    return {
        "p_blocks": bell_draw(seeds[0], (NB, N_COL, KT, BS, BS), (BS * 2 * W) ** -0.5, 0.125, ((0, 16), (1, 4), (2, 2)), jnp.float32),
        "s_blocks": bell_draw(seeds[1], (NB, N_COL, KT, BS, BS), 1.0, 6.0, ((0, 16), (1, 4)), jnp.float32),
        "p_pattern": draw_p_pattern(jax.random.fold_in(seeds[4], 71), 0),
        "s_pattern": draw_s_pattern(jax.random.fold_in(seeds[4], 71), 0),
    }


def reference(p_blocks, s_blocks, p_pattern, s_pattern):
    s_flat = s_blocks.reshape(NB * N_COL * KT, BS, BS)
    slot_ids = jnp.arange(KT, dtype=jnp.int32)
    group_ids = jnp.arange(N_COL, dtype=jnp.int32)

    def one_row(inputs):
        p_row, col_row = inputs
        inner = col_row.reshape(N_COL * KT)
        safe_cols = jnp.maximum(inner, 0)
        s_rows = s_pattern[safe_cols]
        matches = (s_rows[:, :, None, :] == col_row[None, :, :, None]) & (col_row >= 0)[None, :, :, None] & (inner >= 0)[:, None, None, None]
        picked = jnp.sum(jnp.where(matches, slot_ids, 0), axis=3).astype(jnp.int32)
        found = jnp.any(matches, axis=3)
        index = ((safe_cols[:, None, None] * N_COL + group_ids[None, :, None]) * KT + picked).astype(jnp.int32)
        chosen = jnp.where(found[..., None, None], s_flat[index], jnp.zeros((), s_flat.dtype))
        left_blocks = p_row.reshape(N_COL * KT, BS, BS)
        return jnp.einsum('amn,agcnp->gcmp', left_blocks, chosen, precision=lax.Precision.HIGHEST)

    return lax.map(one_row, (p_blocks, p_pattern))
```

```python
import functools

import jax
import jax.numpy as jnp
from jax import lax
from jax.experimental import pallas as pl
from jax.experimental.pallas import tpu as pltpu
from jax.sharding import PartitionSpec as P

BS = 128
W = 10
MESH = pl.DeviceIdType.MESH
BF = jnp.bfloat16


def split(x):
    hi = x.astype(BF)
    return hi, (x - hi.astype(jnp.float32)).astype(BF)


def kernel(
    sizes,
    p_pat,
    s_pat,
    p_in,
    s_in,
    out,
    p_land,
    s_land,
    s_hi,
    s_lo,
    lhs,
    part,
    got,
    mine,
    table,
    p_send,
    p_recv,
    f_send,
    f_recv,
    s_send,
    s_recv,
    x_send,
    x_recv,
    e_send,
    e_recv,
    own_p,
    own_s,
    o_sem,
):
    n_row, n_col, rows, half = sizes
    slots = 2 * half
    total = n_row * rows
    window = 3 * rows
    zero_block = window * slots
    chunks = rows // 2
    r, z, d = lax.axis_index("row"), lax.axis_index("col"), lax.axis_index("depth")
    sib = 1 - d
    row_to = (lax.rem(r + 1, n_row), lax.rem(r + n_row - 1, n_row))
    col_to = (lax.rem(z + 1, n_col), lax.rem(z + n_col - 1, n_col))
    first_row = r * rows

    def p_direct(k, t):
        return pltpu.make_async_remote_copy(
            src_ref=p_in.at[t, 0],
            dst_ref=p_land.at[1 + k, t],
            send_sem=p_send.at[k, t],
            recv_sem=p_recv.at[k, t],
            device_id={"col": col_to[k]},
            device_id_type=MESH,
        )

    def p_forward(k, t):
        return pltpu.make_async_remote_copy(
            src_ref=p_land.at[1 + k, t],
            dst_ref=p_land.at[3, t],
            send_sem=f_send.at[t],
            recv_sem=f_recv.at[t],
            device_id={"col": col_to[k]},
            device_id_type=MESH,
        )

    def s_direct(k, u):
        at = d * chunks + u
        return pltpu.make_async_remote_copy(
            src_ref=s_in.at[at, 0],
            dst_ref=s_land.at[2 * k * rows + at],
            send_sem=s_send.at[k, u],
            recv_sem=s_recv.at[k, u],
            device_id={"row": row_to[k]},
            device_id_type=MESH,
        )

    def s_cross(k, u):
        at = 2 * k * rows + d * chunks + u
        return pltpu.make_async_remote_copy(
            src_ref=s_land.at[at],
            dst_ref=s_land.at[at],
            send_sem=x_send.at[k, u],
            recv_sem=x_recv.at[k, u],
            device_id={"depth": sib},
            device_id_type=MESH,
        )

    def exchange(i):
        return pltpu.make_async_remote_copy(
            src_ref=part.at[i],
            dst_ref=got.at[i],
            send_sem=e_send.at[i],
            recv_sem=e_recv.at[i],
            device_id={"depth": sib},
            device_id_type=MESH,
        )

    def load_s(t):
        return pltpu.make_async_copy(s_in.at[t, 0], s_land.at[rows + t], own_s.at[t])

    def load_p(t):
        return pltpu.make_async_copy(p_in.at[t, 0], p_land.at[0, t], own_p.at[t])

    def store(i):
        return pltpu.make_async_copy(mine.at[i], out.at[i, 0], o_sem.at[i])

    def convert(at):
        for b in range(slots):
            hi, lo = split(s_land[at, b])
            s_hi[at * slots + b] = hi
            s_lo[at * slots + b] = lo

    def index_row(i):
        for q, shift in enumerate((0, n_col - 1, 1, 2)):
            group = lax.rem(z + shift, n_col)
            for a in range(half):
                col = p_pat[(i * n_col + group) * slots + d * half + a]
                safe = jnp.maximum(col, 0)
                at = safe - first_row + W
                at = jnp.where(at < 0, at + total, at)
                at = jnp.where(at >= total, at - total, at)
                at = jnp.clip(at, 0, window - 1)
                have = [s_pat[safe * slots + b] for b in range(slots)]
                for c in range(slots):
                    target = p_pat[(i * n_col + z) * slots + lax.rem(c + d * half, slots)]
                    wanted = jnp.where(col >= 0, target, -1)
                    found = jnp.int32(zero_block)
                    for b in range(slots):
                        found = jnp.where(have[b] == wanted, at * slots + b, found)
                    found = jnp.where(wanted >= 0, found, zero_block)
                    table[(i * n_col * half + q * half + a) * slots + c] = found

    barrier = pltpu.get_barrier_semaphore()
    for k in range(2):
        pl.semaphore_signal(barrier, inc=1, device_id={"row": row_to[k]}, device_id_type=MESH)
        pl.semaphore_signal(barrier, inc=1, device_id={"col": col_to[k]}, device_id_type=MESH)
    pl.semaphore_signal(barrier, inc=1, device_id={"depth": sib}, device_id_type=MESH)
    pl.semaphore_wait(barrier, 5)

    @pl.loop(0, chunks)
    def _(u):
        for k in range(2):
            s_direct(k, u).start()
            for t in range(2):
                p_direct(k, 2 * u + t).start()

    @pl.loop(0, rows)
    def _(t):
        load_s(t).start()
        load_p(t).start()

    s_hi[zero_block] = jnp.zeros((BS, BS), BF)
    s_lo[zero_block] = jnp.zeros((BS, BS), BF)

    @pl.loop(0, chunks)
    def _(u):
        for t in range(2):
            index_row(2 * u + t)
            load_s(2 * u + t).wait()
            load_p(2 * u + t).wait()
            convert(rows + 2 * u + t)
        for t in range(2):
            for k in range(2):
                p_direct(k, 2 * u + t).wait_recv()
        for t in range(2):
            p_forward(t, 2 * u + t).start()
        for k in range(2):
            s_direct(k, u).wait_recv()
            s_cross(k, u).start()
        for k in range(2):
            convert(2 * k * rows + d * chunks + u)
        for k in range(2):
            s_cross(k, u).wait_recv()
            convert(2 * k * rows + sib * chunks + u)

    inner = n_col * half

    def finish(i):
        exchange(i).wait_recv()
        for c in range(half):
            mine[i, c] = mine[i, c] + got[i, c]
        store(i).start()

    @pl.loop(0, rows)
    def _(i):
        p_forward(0, i).wait_recv()
        for n in range(inner):
            hi, lo = split(p_land[n // half, i, n % half])
            lhs[0, :, n * BS : (n + 1) * BS] = hi
            lhs[1, :, n * BS : (n + 1) * BS] = lo
        for tile in reversed(range(slots // 2)):
            acc = jnp.zeros((BS, 2 * BS), jnp.float32)
            for pair in range(inner // 2):
                where = [
                    [
                        table[(i * inner + 2 * pair + n) * slots + 2 * tile + c]
                        for c in range(2)
                    ]
                    for n in range(2)
                ]

                def blocks(ref):
                    return jnp.concatenate(
                        [jnp.concatenate([ref[w] for w in line], axis=1) for line in where],
                        axis=0,
                    )

                cols = slice(2 * pair * BS, 2 * (pair + 1) * BS)
                right_hi, right_lo = blocks(s_hi), blocks(s_lo)
                acc += jnp.dot(lhs[0, :, cols], right_hi, preferred_element_type=jnp.float32)
                acc += jnp.dot(lhs[1, :, cols], right_hi, preferred_element_type=jnp.float32)
                acc += jnp.dot(lhs[0, :, cols], right_lo, preferred_element_type=jnp.float32)
            for c in range(2):
                slot = 2 * tile + c
                value = acc[:, c * BS : (c + 1) * BS]
                if slot < half:
                    mine[i, slot] = value
                else:
                    part[i, slot - half] = value
        exchange(i).start()

        @pl.when(i > 0)
        def _():
            finish(i - 1)

    finish(rows - 1)

    @pl.loop(0, rows)
    def _(i):
        store(i).wait()
        exchange(i).wait_send()
        p_forward(0, i).wait_send()
        for k in range(2):
            p_direct(k, i).wait_send()

    @pl.loop(0, chunks)
    def _(u):
        for k in range(2):
            s_direct(k, u).wait_send()
            s_cross(k, u).wait_send()


def per_device(p_blocks, s_blocks, p_pattern, s_pattern):
    rows, _, half = p_blocks.shape[:3]
    n_row, n_col = lax.axis_size("row"), lax.axis_size("col")
    slots = 2 * half
    f32 = jnp.float32
    dma = pltpu.SemaphoreType.DMA
    chunks = rows // 2
    return pl.pallas_call(
        functools.partial(kernel, (n_row, n_col, rows, half)),
        out_shape=jax.ShapeDtypeStruct(p_blocks.shape, f32),
        in_specs=[pl.BlockSpec(memory_space=pltpu.SMEM)] * 2
        + [pl.BlockSpec(memory_space=pl.ANY)] * 2,
        out_specs=pl.BlockSpec(memory_space=pl.ANY),
        scratch_shapes=[
            pltpu.VMEM((4, rows, half, BS, BS), f32),
            pltpu.VMEM((3 * rows, slots, BS, BS), f32),
            pltpu.VMEM((3 * rows * slots + 1, BS, BS), BF),
            pltpu.VMEM((3 * rows * slots + 1, BS, BS), BF),
            pltpu.VMEM((2, BS, n_col * half * BS), BF),
            pltpu.VMEM((rows, half, BS, BS), f32),
            pltpu.VMEM((rows, half, BS, BS), f32),
            pltpu.VMEM((rows, half, BS, BS), f32),
            pltpu.SMEM((rows * n_col * half * slots,), jnp.int32),
            dma((2, rows)),
            dma((2, rows)),
            dma((rows,)),
            dma((rows,)),
            dma((2, chunks)),
            dma((2, chunks)),
            dma((2, chunks)),
            dma((2, chunks)),
            dma((rows,)),
            dma((rows,)),
            dma((rows,)),
            dma((rows,)),
            dma((rows,)),
        ],
        compiler_params=pltpu.CompilerParams(
            collective_id=0, has_side_effects=True, vmem_limit_bytes=56 * 2**20
        ),
        cost_estimate=pl.CostEstimate(
            flops=9 * 10**9, bytes_accessed=10**7, transcendentals=0
        ),
    )(p_pattern.reshape(-1), s_pattern.reshape(-1), p_blocks, s_blocks)


def solution(mesh):
    in_specs = (
        P("row", "col", "depth", None, None),
        P("row", "col", None, None, None),
        P("row", None, None),
        P(None, "col", None),
    )
    out_specs = P("row", "col", "depth", None, None)
    return jax.shard_map(
        per_device, mesh=mesh, in_specs=in_specs, out_specs=out_specs, check_vma=False
    )
```

```python
import functools

import jax
import jax.numpy as jnp
from jax import lax
from jax.experimental import pallas as pl
from jax.experimental.pallas import tpu as pltpu
from jax.sharding import PartitionSpec as P

BS = 128
W = 10
MESH = pl.DeviceIdType.MESH
BF = jnp.bfloat16


def split(x):
    hi = x.astype(BF)
    return hi, (x - hi.astype(jnp.float32)).astype(BF)


def kernel(
    sizes,
    p_pat_in,
    s_pat_in,
    p_in,
    s_in,
    out,
    p_pat,
    s_pat,
    p_land,
    s_land,
    s_hi,
    s_lo,
    lhs,
    sums,
    part,
    got,
    table,
    p_send,
    p_recv,
    f_send,
    f_recv,
    s_send,
    s_recv,
    x_send,
    x_recv,
    e_send,
    e_recv,
    own_p,
    own_s,
    pat_sem,
):
    n_row, n_col, rows, half = sizes
    slots = 2 * half
    total = n_row * rows
    window = 3 * rows
    zero_block = window * slots
    chunks = rows // 2
    r, z, d = lax.axis_index("row"), lax.axis_index("col"), lax.axis_index("depth")
    sib = 1 - d
    row_to = (lax.rem(r + 1, n_row), lax.rem(r + n_row - 1, n_row))
    col_to = (lax.rem(z + 1, n_col), lax.rem(z + n_col - 1, n_col))
    first_row = r * rows

    def p_direct(k, t):
        return pltpu.make_async_remote_copy(
            src_ref=p_in.at[t, 0],
            dst_ref=p_land.at[1 + k, t],
            send_sem=p_send.at[k, t],
            recv_sem=p_recv.at[k, t],
            device_id={"col": col_to[k]},
            device_id_type=MESH,
        )

    def p_forward(k, t):
        piece = pl.ds(k * half * BS // 2, half * BS // 2)
        return pltpu.make_async_remote_copy(
            src_ref=p_land.at[1 + k, t, piece],
            dst_ref=p_land.at[3, t, piece],
            send_sem=f_send.at[k, t],
            recv_sem=f_recv.at[k, t],
            device_id={"col": col_to[k]},
            device_id_type=MESH,
        )

    def s_direct(k, u):
        at = d * chunks + u
        return pltpu.make_async_remote_copy(
            src_ref=s_in.at[at, 0],
            dst_ref=s_land.at[2 * k * rows + at],
            send_sem=s_send.at[k, u],
            recv_sem=s_recv.at[k, u],
            device_id={"row": row_to[k]},
            device_id_type=MESH,
        )

    def s_cross(k, u):
        at = 2 * k * rows + d * chunks + u
        return pltpu.make_async_remote_copy(
            src_ref=s_land.at[at],
            dst_ref=s_land.at[at],
            send_sem=x_send.at[k, u],
            recv_sem=x_recv.at[k, u],
            device_id={"depth": sib},
            device_id_type=MESH,
        )

    def exchange(i):
        return pltpu.make_async_remote_copy(
            src_ref=part.at[i],
            dst_ref=got.at[i],
            send_sem=e_send.at[i],
            recv_sem=e_recv.at[i],
            device_id={"depth": sib},
            device_id_type=MESH,
        )

    def load_s(t):
        return pltpu.make_async_copy(s_in.at[t, 0], s_land.at[rows + t], own_s.at[t])

    def load_p(t):
        return pltpu.make_async_copy(p_in.at[t, 0], p_land.at[0, t], own_p.at[t])

    def convert(at):
        for b in range(slots):
            hi, lo = split(s_land[at, b])
            s_hi[at * slots + b] = hi
            s_lo[at * slots + b] = lo

    def index_row(i):
        for q, shift in enumerate((0, n_col - 1, 1, 2)):
            group = lax.rem(z + shift, n_col)
            for a in range(half):
                col = p_pat[d * half + a, group, i]
                safe = jnp.maximum(col, 0)
                at = safe - first_row + W
                at = jnp.where(at < 0, at + total, at)
                at = jnp.where(at >= total, at - total, at)
                at = jnp.clip(at, 0, window - 1)
                have = [s_pat[b, 0, safe] for b in range(slots)]
                for c in range(slots):
                    target = p_pat[lax.rem(c + d * half, slots), z, i]
                    wanted = jnp.where(col >= 0, target, -1)
                    found = jnp.int32(zero_block)
                    for b in range(slots):
                        found = jnp.where(have[b] == wanted, at * slots + b, found)
                    found = jnp.where(wanted >= 0, found, zero_block)
                    table[(i * n_col * half + q * half + a) * slots + c] = found

    barrier = pltpu.get_barrier_semaphore()
    for k in range(2):
        pl.semaphore_signal(barrier, inc=1, device_id={"row": row_to[k]}, device_id_type=MESH)
        pl.semaphore_signal(barrier, inc=1, device_id={"col": col_to[k]}, device_id_type=MESH)
    pl.semaphore_signal(barrier, inc=1, device_id={"depth": sib}, device_id_type=MESH)
    pl.semaphore_wait(barrier, 5)

    @pl.loop(0, rows)
    def _(t):
        for k in range(2):
            p_direct(k, t).start()

    @pl.loop(0, chunks)
    def _(u):
        for k in range(2):
            s_direct(k, u).start()

    patterns = [
        pltpu.make_async_copy(p_pat_in, p_pat, pat_sem.at[0]),
        pltpu.make_async_copy(s_pat_in, s_pat, pat_sem.at[1]),
    ]
    for copy in patterns:
        copy.start()

    @pl.loop(0, rows)
    def _(t):
        load_s(t).start()
        load_p(t).start()

    for copy in patterns:
        copy.wait()
    s_hi[zero_block] = jnp.zeros((BS, BS), BF)
    s_lo[zero_block] = jnp.zeros((BS, BS), BF)

    @pl.loop(0, chunks)
    def _(u):
        for t in range(2):
            index_row(2 * u + t)
            load_s(2 * u + t).wait()
            load_p(2 * u + t).wait()
            convert(rows + 2 * u + t)
        for t in range(2):
            for k in range(2):
                p_direct(k, 2 * u + t).wait_recv()
        for t in range(2):
            for k in range(2):
                p_forward(k, 2 * u + t).start()
        for k in range(2):
            s_direct(k, u).wait_recv()
            s_cross(k, u).start()
        for k in range(2):
            convert(2 * k * rows + d * chunks + u)
        for k in range(2):
            s_cross(k, u).wait_recv()
            convert(2 * k * rows + sib * chunks + u)

    inner = n_col * half

    def finish(i):
        exchange(i).wait_recv()
        for c in range(half):
            out[i, 0, c] = out[i, 0, c] + got[i, c]

    early = 8

    def spread(i, first, last):
        for n in range(first, last):
            block = slice(n % half * BS, (n % half + 1) * BS)
            hi, lo = split(p_land[n // half, i, block])
            lhs[0, :, n * BS : (n + 1) * BS] = hi
            lhs[1, :, n * BS : (n + 1) * BS] = lo

    def multiply(i, tile, first, last, acc):
        for n in range(first, last, 2):
            where = [
                [table[(i * inner + m) * slots + 2 * tile + c] for c in range(2)]
                for m in (n, n + 1)
            ]

            def blocks(ref):
                return jnp.concatenate(
                    [jnp.concatenate([ref[w] for w in line], axis=1) for line in where],
                    axis=0,
                )

            cols = slice(n * BS, (n + 2) * BS)
            right_hi, right_lo = blocks(s_hi), blocks(s_lo)
            for left, right in ((0, right_hi), (1, right_hi), (0, right_lo)):
                term = jnp.dot(
                    lhs[left, :, cols], right, preferred_element_type=jnp.float32
                )
                acc = term if acc is None else acc + term
        return acc

    @pl.loop(0, rows)
    def _(i):
        spread(i, 0, 3 * half)
        for tile in range(slots // 2):
            sums[tile] = multiply(i, tile, 0, early, None)

        @pl.when(i > 0)
        def _():
            finish(i - 1)

        for k in range(2):
            p_direct(k, i).wait_send()
            p_forward(k, i).wait_recv()
        spread(i, 3 * half, inner)
        for tile in reversed(range(slots // 2)):
            acc = multiply(i, tile, early, inner, sums[tile])
            for c in range(2):
                slot = 2 * tile + c
                value = acc[:, c * BS : (c + 1) * BS]
                if slot < half:
                    out[i, 0, slot] = value
                else:
                    part[i, slot - half] = value
            if tile == half // 2:
                exchange(i).start()

        @pl.when(i < chunks)
        def _():
            for k in range(2):
                s_direct(k, i).wait_send()
                s_cross(k, i).wait_send()

        @pl.when(i > 0)
        def _():
            exchange(i - 1).wait_send()
            for k in range(2):
                p_forward(k, i - 1).wait_send()

    finish(rows - 1)
    exchange(rows - 1).wait_send()
    for k in range(2):
        p_forward(k, rows - 1).wait_send()


def per_device(p_blocks, s_blocks, p_pattern, s_pattern):
    rows, _, half = p_blocks.shape[:3]
    n_row, n_col = lax.axis_size("row"), lax.axis_size("col")
    slots = 2 * half
    f32 = jnp.float32
    dma = pltpu.SemaphoreType.DMA
    chunks = rows // 2
    return pl.pallas_call(
        functools.partial(kernel, (n_row, n_col, rows, half)),
        out_shape=pltpu.VMEM(p_blocks.shape, f32),
        in_specs=[pl.BlockSpec(memory_space=pl.ANY)] * 4,
        out_specs=pl.BlockSpec(memory_space=pltpu.VMEM),
        scratch_shapes=[
            pltpu.SMEM((slots, n_col, rows), jnp.int32),
            pltpu.SMEM((slots, 1, n_row * rows), jnp.int32),
            pltpu.VMEM((4, rows, half * BS, BS), f32),
            pltpu.VMEM((3 * rows, slots, BS, BS), f32),
            pltpu.VMEM((3 * rows * slots + 1, BS, BS), BF),
            pltpu.VMEM((3 * rows * slots + 1, BS, BS), BF),
            pltpu.VMEM((2, BS, n_col * half * BS), BF),
            pltpu.VMEM((half, BS, 2 * BS), f32),
            pltpu.VMEM((rows, half, BS, BS), f32),
            pltpu.VMEM((rows, half, BS, BS), f32),
            pltpu.SMEM((rows * n_col * half * slots,), jnp.int32),
            dma((2, rows)),
            dma((2, rows)),
            dma((2, rows)),
            dma((2, rows)),
            dma((2, chunks)),
            dma((2, chunks)),
            dma((2, chunks)),
            dma((2, chunks)),
            dma((rows,)),
            dma((rows,)),
            dma((rows,)),
            dma((rows,)),
            dma((2,)),
        ],
        compiler_params=pltpu.CompilerParams(
            collective_id=0, has_side_effects=True, vmem_limit_bytes=56 * 2**20
        ),
        cost_estimate=pl.CostEstimate(
            flops=9 * 10**9, bytes_accessed=10**7, transcendentals=0
        ),
    )(
        jnp.transpose(p_pattern, (2, 1, 0)),
        jnp.transpose(s_pattern, (2, 1, 0)),
        p_blocks.reshape(rows, 1, half * BS, BS),
        s_blocks,
    )


def solution(mesh):
    in_specs = (
        P("row", "col", "depth", None, None),
        P("row", "col", None, None, None),
        P("row", None, None),
        P(None, "col", None),
    )
    out_specs = P("row", "col", "depth", None, None)
    return jax.shard_map(
        per_device, mesh=mesh, in_specs=in_specs, out_specs=out_specs, check_vma=False
    )
```

```python
import functools

import jax
import jax.numpy as jnp
from jax import lax
from jax.experimental import pallas as pl
from jax.experimental.pallas import tpu as pltpu
from jax.sharding import PartitionSpec as P

BS = 128
W = 10
MESH = pl.DeviceIdType.MESH
BF = jnp.bfloat16


def split(x):
    hi = x.astype(BF)
    return hi, (x - hi.astype(jnp.float32)).astype(BF)


def kernel(
    sizes,
    p_pat_in,
    s_pat_in,
    p_in,
    s_in,
    out,
    p_pat,
    s_pat,
    p_land,
    s_land,
    s_hi,
    s_lo,
    lhs,
    sums,
    part,
    got,
    table,
    p_send,
    p_recv,
    f_send,
    f_recv,
    s_send,
    s_recv,
    x_send,
    x_recv,
    e_send,
    e_recv,
    own_p,
    own_s,
    pat_sem,
):
    n_row, n_col, rows, half = sizes
    slots = 2 * half
    total = n_row * rows
    window = 3 * rows
    zero_block = window * slots
    chunks = rows // 2
    r, z, d = lax.axis_index("row"), lax.axis_index("col"), lax.axis_index("depth")
    sib = 1 - d
    row_to = (lax.rem(r + 1, n_row), lax.rem(r + n_row - 1, n_row))
    col_to = (lax.rem(z + 1, n_col), lax.rem(z + n_col - 1, n_col))
    first_row = r * rows

    def p_direct(k, t, count=2):
        return pltpu.make_async_remote_copy(
            src_ref=p_in.at[pl.ds(2 * t, count)],
            dst_ref=p_land.at[1 + k, pl.ds(2 * t, count)],
            send_sem=p_send.at[k],
            recv_sem=p_recv.at[k, t],
            device_id={"col": col_to[k]},
            device_id_type=MESH,
        )

    def p_forward(k, t, count=1):
        lines = half * BS // 2
        at = (pl.ds(t, count), pl.ds(k * lines, lines))
        return pltpu.make_async_remote_copy(
            src_ref=p_land.at[1 + k, *at],
            dst_ref=p_land.at[3, *at],
            send_sem=f_send.at[k],
            recv_sem=f_recv.at[t],
            device_id={"col": col_to[k]},
            device_id_type=MESH,
        )

    def p_forwarded(t):
        return pltpu.make_async_remote_copy(
            src_ref=p_land.at[1, t],
            dst_ref=p_land.at[3, t],
            send_sem=f_send.at[0],
            recv_sem=f_recv.at[t],
            device_id={"col": col_to[0]},
            device_id_type=MESH,
        )

    def s_direct(k, u, count=1):
        at = d * chunks + u
        return pltpu.make_async_remote_copy(
            src_ref=s_in.at[pl.ds(at, count), 0],
            dst_ref=s_land.at[pl.ds(2 * k * rows + at, count)],
            send_sem=s_send.at[k],
            recv_sem=s_recv.at[k, u],
            device_id={"row": row_to[k]},
            device_id_type=MESH,
        )

    def s_cross(k, u, count=1):
        at = pl.ds(2 * k * rows + d * chunks + u, count)
        return pltpu.make_async_remote_copy(
            src_ref=s_land.at[at],
            dst_ref=s_land.at[at],
            send_sem=x_send.at[k],
            recv_sem=x_recv.at[k, u],
            device_id={"depth": sib},
            device_id_type=MESH,
        )

    def exchange(i, first=0, count=half, lines=1):
        at = (pl.ds(i, lines), pl.ds(first, count))
        return pltpu.make_async_remote_copy(
            src_ref=part.at[*at],
            dst_ref=got.at[*at],
            send_sem=e_send,
            recv_sem=e_recv.at[i],
            device_id={"depth": sib},
            device_id_type=MESH,
        )

    def load_s(u):
        at = pl.ds(2 * u, 2)
        return pltpu.make_async_copy(
            s_in.at[at, 0], s_land.at[pl.ds(rows + 2 * u, 2)], own_s.at[u]
        )

    def convert(at):
        for b in range(slots):
            hi, lo = split(s_land[at, b])
            s_hi[at * slots + b] = hi
            s_lo[at * slots + b] = lo

    def index_row(i):
        for q, shift in enumerate((0, n_col - 1, 1, 2)):
            group = lax.rem(z + shift, n_col)
            for a in range(half):
                col = p_pat[d * half + a, group, i]
                safe = jnp.maximum(col, 0)
                at = safe - first_row + W
                at = jnp.where(at < 0, at + total, at)
                at = jnp.where(at >= total, at - total, at)
                at = jnp.clip(at, 0, window - 1)
                have = [s_pat[b, 0, safe] for b in range(slots)]
                for c in range(slots):
                    target = p_pat[lax.rem(c + d * half, slots), z, i]
                    wanted = jnp.where(col >= 0, target, -1)
                    found = jnp.int32(zero_block)
                    for b in range(slots):
                        found = jnp.where(have[b] == wanted, at * slots + b, found)
                    found = jnp.where(wanted >= 0, found, zero_block)
                    table[(i * n_col * half + q * half + a) * slots + c] = found

    barrier = pltpu.get_barrier_semaphore()
    for k in range(2):
        pl.semaphore_signal(barrier, inc=1, device_id={"row": row_to[k]}, device_id_type=MESH)
        pl.semaphore_signal(barrier, inc=1, device_id={"col": col_to[k]}, device_id_type=MESH)
    pl.semaphore_signal(barrier, inc=1, device_id={"depth": sib}, device_id_type=MESH)
    pl.semaphore_wait(barrier, 5)

    for start in (p_direct, s_direct):

        @pl.loop(0, chunks)
        def _(u):
            for k in range(2):
                start(k, u).start()

    patterns = [
        pltpu.make_async_copy(p_pat_in, p_pat, pat_sem.at[0]),
        pltpu.make_async_copy(s_pat_in, s_pat, pat_sem.at[1]),
    ]
    for copy in patterns:
        copy.start()

    load_p = pltpu.make_async_copy(p_in, p_land.at[0], own_p)
    load_p.start()

    @pl.loop(0, chunks)
    def _(u):
        load_s(u).start()

    for copy in patterns:
        copy.wait()
    s_hi[zero_block] = jnp.zeros((BS, BS), BF)
    s_lo[zero_block] = jnp.zeros((BS, BS), BF)

    @pl.loop(0, chunks)
    def _(u):
        for t in range(2):
            index_row(2 * u + t)
        load_s(u).wait()
        for t in range(2):
            convert(rows + 2 * u + t)
        for k in range(2):
            p_direct(k, u).wait_recv()
        for t in range(2):
            for k in range(2):
                p_forward(k, 2 * u + t).start()
        for k in range(2):
            s_direct(k, u).wait_recv()
            s_cross(k, u).start()
        for k in range(2):
            convert(2 * k * rows + d * chunks + u)
        for k in range(2):
            s_cross(k, u).wait_recv()
            convert(2 * k * rows + sib * chunks + u)

    inner = n_col * half

    def finish(i):
        exchange(i).wait_recv()
        for c in range(half):
            out[i, 0, c] = out[i, 0, c] + got[i, c]

    direct = 3 * half
    load_p.wait()

    def spread(i, first, last):
        for n in range(first, last):
            block = slice(n % half * BS, (n % half + 1) * BS)
            hi, lo = split(p_land[n // half, i, block])
            lhs[0, :, n * BS : (n + 1) * BS] = hi
            lhs[1, :, n * BS : (n + 1) * BS] = lo

    def multiply(i, tile, first, last, acc):
        terms = [
            (left, right, n)
            for left, right in ((0, s_hi), (1, s_hi), (0, s_lo))
            for n in range(first, last)
        ]
        for at in range(0, len(terms), 2):
            pair = terms[at : at + 2]
            wide = jnp.concatenate(
                [lhs[left, :, n * BS : (n + 1) * BS] for left, _, n in pair], axis=1
            )
            deep = jnp.concatenate(
                [
                    jnp.concatenate(
                        [
                            right[table[(i * inner + n) * slots + 2 * tile + c]]
                            for c in range(2)
                        ],
                        axis=1,
                    )
                    for _, right, n in pair
                ],
                axis=0,
            )
            term = jnp.dot(wide, deep, preferred_element_type=jnp.float32)
            acc = term if acc is None else acc + term
        return acc

    @pl.loop(0, rows)
    def _(i):
        spread(i, 0, direct)
        for tile in range(slots // 2):
            sums[i, tile] = multiply(i, tile, 0, direct, None)

    for k in range(2):
        p_direct(k, 0, rows).wait_send()
        s_direct(k, 0, chunks).wait_send()
        s_cross(k, 0, chunks).wait_send()

    @pl.loop(0, rows)
    def _(i):
        p_forwarded(i).wait_recv()
        spread(i, direct, inner)
        for tile in reversed(range(slots // 2)):
            acc = multiply(i, tile, direct, inner, sums[i, tile])
            for c in range(2):
                slot = 2 * tile + c
                value = acc[:, c * BS : (c + 1) * BS]
                if slot < half:
                    out[i, 0, slot] = value
                else:
                    part[i, slot - half] = value
            if tile == 2:
                exchange(i, 1, 2).start()
            if tile == 1:
                exchange(i, 0, 1).start()

        @pl.when(i > 0)
        def _():
            finish(i - 1)

    for k in range(2):
        p_forward(k, 0, rows).wait_send()
    finish(rows - 1)
    exchange(0, lines=rows).wait_send()


def per_device(p_blocks, s_blocks, p_pattern, s_pattern):
    rows, _, half = p_blocks.shape[:3]
    n_row, n_col = lax.axis_size("row"), lax.axis_size("col")
    slots = 2 * half
    f32 = jnp.float32
    dma = pltpu.SemaphoreType.DMA
    chunks = rows // 2
    return pl.pallas_call(
        functools.partial(kernel, (n_row, n_col, rows, half)),
        out_shape=pltpu.VMEM(p_blocks.shape, f32),
        in_specs=[pl.BlockSpec(memory_space=pl.ANY)] * 4,
        out_specs=pl.BlockSpec(memory_space=pltpu.VMEM),
        scratch_shapes=[
            pltpu.SMEM((slots, n_col, rows), jnp.int32),
            pltpu.SMEM((slots, 1, n_row * rows), jnp.int32),
            pltpu.VMEM((4, rows, half * BS, BS), f32),
            pltpu.VMEM((3 * rows, slots, BS, BS), f32),
            pltpu.VMEM((3 * rows * slots + 1, BS, BS), BF),
            pltpu.VMEM((3 * rows * slots + 1, BS, BS), BF),
            pltpu.VMEM((2, BS, n_col * half * BS), BF),
            pltpu.VMEM((rows, half, BS, 2 * BS), f32),
            pltpu.VMEM((rows, half, BS, BS), f32),
            pltpu.VMEM((rows, half, BS, BS), f32),
            pltpu.SMEM((rows * n_col * half * slots,), jnp.int32),
            dma((2,)),
            dma((2, chunks)),
            dma((2,)),
            dma((rows,)),
            dma((2,)),
            dma((2, chunks)),
            dma((2,)),
            dma((2, chunks)),
            dma,
            dma((rows,)),
            dma,
            dma((chunks,)),
            dma((2,)),
        ],
        compiler_params=pltpu.CompilerParams(
            collective_id=0, has_side_effects=True, vmem_limit_bytes=56 * 2**20
        ),
        cost_estimate=pl.CostEstimate(
            flops=9 * 10**9, bytes_accessed=10**7, transcendentals=0
        ),
    )(
        jnp.transpose(p_pattern, (2, 1, 0)),
        jnp.transpose(s_pattern, (2, 1, 0)),
        p_blocks.reshape(rows, half * BS, BS),
        s_blocks,
    )


def solution(mesh):
    in_specs = (
        P("row", "col", "depth", None, None),
        P("row", "col", None, None, None),
        P("row", None, None),
        P(None, "col", None),
    )
    out_specs = P("row", "col", "depth", None, None)
    return jax.shard_map(
        per_device, mesh=mesh, in_specs=in_specs, out_specs=out_specs, check_vma=False
    )
```

```python
import functools

import jax
import jax.numpy as jnp
from jax import lax
from jax.experimental import pallas as pl
from jax.experimental.pallas import tpu as pltpu
from jax.sharding import PartitionSpec as P

BS = 128
W = 10
MESH = pl.DeviceIdType.MESH
BF = jnp.bfloat16


def split(x):
    hi = x.astype(BF)
    return hi, (x - hi.astype(jnp.float32)).astype(BF)


def kernel(
    sizes,
    p_pat_in,
    s_pat_in,
    p_in,
    s_in,
    out,
    p_pat,
    s_pat,
    p_land,
    s_land,
    s_hi,
    s_lo,
    lhs,
    sums,
    part,
    got,
    table,
    p_send,
    p_recv,
    f_send,
    f_recv,
    s_send,
    s_recv,
    x_send,
    x_recv,
    e_send,
    e_recv,
    own_p,
    own_s,
    pat_sem,
):
    n_row, n_col, rows, half = sizes
    slots = 2 * half
    total = n_row * rows
    window = 3 * rows
    zero_block = window * slots
    chunks = rows // 2
    r, z, d = lax.axis_index("row"), lax.axis_index("col"), lax.axis_index("depth")
    sib = 1 - d
    row_to = (lax.rem(r + 1, n_row), lax.rem(r + n_row - 1, n_row))
    col_to = (lax.rem(z + 1, n_col), lax.rem(z + n_col - 1, n_col))
    first_row = r * rows

    def p_direct(k, t, count=2):
        return pltpu.make_async_remote_copy(
            src_ref=p_in.at[pl.ds(2 * t, count)],
            dst_ref=p_land.at[1 + k, pl.ds(2 * t, count)],
            send_sem=p_send.at[k],
            recv_sem=p_recv.at[k, t],
            device_id={"col": col_to[k]},
            device_id_type=MESH,
        )

    def p_forward(k, t, count=1):
        lines = half * BS // 2
        at = (pl.ds(t, count), pl.ds(k * lines, lines))
        return pltpu.make_async_remote_copy(
            src_ref=p_land.at[1 + k, *at],
            dst_ref=p_land.at[3, *at],
            send_sem=f_send.at[k],
            recv_sem=f_recv.at[t],
            device_id={"col": col_to[k]},
            device_id_type=MESH,
        )

    def p_forwarded(t):
        return pltpu.make_async_remote_copy(
            src_ref=p_land.at[1, t],
            dst_ref=p_land.at[3, t],
            send_sem=f_send.at[0],
            recv_sem=f_recv.at[t],
            device_id={"col": col_to[0]},
            device_id_type=MESH,
        )

    def s_direct(k, u, count=1):
        at = d * chunks + u
        return pltpu.make_async_remote_copy(
            src_ref=s_in.at[pl.ds(at, count), 0],
            dst_ref=s_land.at[pl.ds(2 * k * rows + at, count)],
            send_sem=s_send.at[k],
            recv_sem=s_recv.at[k, u],
            device_id={"row": row_to[k]},
            device_id_type=MESH,
        )

    def s_cross(k, u, count=1):
        at = pl.ds(2 * k * rows + d * chunks + u, count)
        return pltpu.make_async_remote_copy(
            src_ref=s_land.at[at],
            dst_ref=s_land.at[at],
            send_sem=x_send.at[k],
            recv_sem=x_recv.at[k, u],
            device_id={"depth": sib},
            device_id_type=MESH,
        )

    def exchange(i, first=0, count=half, lines=1):
        at = (pl.ds(i, lines), pl.ds(first, count))
        return pltpu.make_async_remote_copy(
            src_ref=part.at[*at],
            dst_ref=got.at[*at],
            send_sem=e_send,
            recv_sem=e_recv.at[i],
            device_id={"depth": sib},
            device_id_type=MESH,
        )

    def load_s(u):
        at = pl.ds(2 * u, 2)
        return pltpu.make_async_copy(
            s_in.at[at, 0], s_land.at[pl.ds(rows + 2 * u, 2)], own_s.at[u]
        )

    def convert(at):
        for b in range(slots):
            hi, lo = split(s_land[at, b])
            s_hi[at * slots + b] = hi
            s_lo[at * slots + b] = lo

    def index_row(i):
        for q, shift in enumerate((0, n_col - 1, 1, 2)):
            group = lax.rem(z + shift, n_col)
            for a in range(half):
                col = p_pat[d * half + a, group, i]
                safe = jnp.maximum(col, 0)
                at = safe - first_row + W
                at = jnp.where(at < 0, at + total, at)
                at = jnp.where(at >= total, at - total, at)
                at = jnp.clip(at, 0, window - 1)
                have = [s_pat[b, 0, safe] for b in range(slots)]
                for c in range(slots):
                    target = p_pat[lax.rem(c + d * half, slots), z, i]
                    wanted = jnp.where(col >= 0, target, -1)
                    found = jnp.int32(zero_block)
                    for b in range(slots):
                        found = jnp.where(have[b] == wanted, at * slots + b, found)
                    found = jnp.where(wanted >= 0, found, zero_block)
                    table[(i * n_col * half + q * half + a) * slots + c] = found

    barrier = pltpu.get_barrier_semaphore()
    for k in range(2):
        pl.semaphore_signal(barrier, inc=1, device_id={"row": row_to[k]}, device_id_type=MESH)
        pl.semaphore_signal(barrier, inc=1, device_id={"col": col_to[k]}, device_id_type=MESH)
    pl.semaphore_signal(barrier, inc=1, device_id={"depth": sib}, device_id_type=MESH)
    pl.semaphore_wait(barrier, 5)

    for start in (p_direct, s_direct):

        @pl.loop(0, chunks)
        def _(u):
            for k in range(2):
                start(k, u).start()

    patterns = [
        pltpu.make_async_copy(p_pat_in, p_pat, pat_sem.at[0]),
        pltpu.make_async_copy(s_pat_in, s_pat, pat_sem.at[1]),
    ]
    for copy in patterns:
        copy.start()

    load_p = pltpu.make_async_copy(p_in, p_land.at[0], own_p)
    load_p.start()

    @pl.loop(0, chunks)
    def _(u):
        load_s(u).start()

    for copy in patterns:
        copy.wait()
    s_hi[zero_block] = jnp.zeros((BS, BS), BF)
    s_lo[zero_block] = jnp.zeros((BS, BS), BF)

    @pl.loop(0, chunks)
    def _(u):
        for t in range(2):
            index_row(2 * u + t)
        load_s(u).wait()
        for t in range(2):
            convert(rows + 2 * u + t)

    def pass_on(u):
        for k in range(2):
            p_direct(k, u).wait_recv()
        for t in range(2):
            for k in range(2):
                p_forward(k, 2 * u + t).start()

    @pl.loop(0, chunks)
    def _(u):
        for k in range(2):
            s_direct(k, u).wait_recv()
            s_cross(k, u).start()
        for k in range(2):
            convert(2 * k * rows + d * chunks + u)
        for k in range(2):
            s_cross(k, u).wait_recv()
            convert(2 * k * rows + sib * chunks + u)

        @pl.when(u < chunks - 1)
        def _():
            pass_on(u)

    inner = n_col * half

    def finish(i):
        exchange(i).wait_recv()
        for c in range(half):
            out[i, 0, c] = out[i, 0, c] + got[i, c]

    direct = 3 * half
    load_p.wait()

    def spread(i, first, last):
        for n in range(first, last):
            block = slice(n % half * BS, (n % half + 1) * BS)
            hi, lo = split(p_land[n // half, i, block])
            lhs[0, :, n * BS : (n + 1) * BS] = hi
            lhs[1, :, n * BS : (n + 1) * BS] = lo

    def multiply(i, tile, first, last, acc):
        terms = [
            (left, right, n)
            for left, right in ((0, s_hi), (1, s_hi), (0, s_lo))
            for n in range(first, last)
        ]
        for at in range(0, len(terms), 2):
            pair = terms[at : at + 2]
            wide = jnp.concatenate(
                [lhs[left, :, n * BS : (n + 1) * BS] for left, _, n in pair], axis=1
            )
            deep = jnp.concatenate(
                [
                    jnp.concatenate(
                        [
                            right[table[(i * inner + n) * slots + 2 * tile + c]]
                            for c in range(2)
                        ],
                        axis=1,
                    )
                    for _, right, n in pair
                ],
                axis=0,
            )
            term = jnp.dot(wide, deep, preferred_element_type=jnp.float32)
            acc = term if acc is None else acc + term
        return acc

    def begin(i):
        spread(i, 0, direct)
        for tile in range(slots // 2):
            sums[i, tile] = multiply(i, tile, 0, direct, None)

    def complete(i):
        p_forwarded(i).wait_recv()
        spread(i, direct, inner)
        for tile in reversed(range(slots // 2)):
            acc = multiply(i, tile, direct, inner, sums[i, tile])
            for c in range(2):
                slot = 2 * tile + c
                value = acc[:, c * BS : (c + 1) * BS]
                if slot < half:
                    out[i, 0, slot] = value
                else:
                    part[i, slot - half] = value
            if tile == 2:
                exchange(i, 1, 2).start()
            if tile == 1:
                exchange(i, 0, 1).start()

    @pl.loop(0, rows + 1)
    def _(j):
        @pl.when(j == 5)
        def _():
            pass_on(chunks - 1)

        @pl.when(j < rows)
        def _():
            begin(j)

        @pl.when(j == rows - 1)
        def _():
            for k in range(2):
                p_direct(k, 0, rows).wait_send()
                s_direct(k, 0, chunks).wait_send()
                s_cross(k, 0, chunks).wait_send()

        @pl.when(j > 0)
        def _():
            complete(j - 1)

        @pl.when(j > 1)
        def _():
            finish(j - 2)

    for k in range(2):
        p_forward(k, 0, rows).wait_send()
    finish(rows - 1)
    exchange(0, lines=rows).wait_send()


def per_device(p_blocks, s_blocks, p_pattern, s_pattern):
    rows, _, half = p_blocks.shape[:3]
    n_row, n_col = lax.axis_size("row"), lax.axis_size("col")
    slots = 2 * half
    f32 = jnp.float32
    dma = pltpu.SemaphoreType.DMA
    chunks = rows // 2
    return pl.pallas_call(
        functools.partial(kernel, (n_row, n_col, rows, half)),
        out_shape=pltpu.VMEM(p_blocks.shape, f32),
        in_specs=[pl.BlockSpec(memory_space=pl.ANY)] * 4,
        out_specs=pl.BlockSpec(memory_space=pltpu.VMEM),
        scratch_shapes=[
            pltpu.SMEM((slots, n_col, rows), jnp.int32),
            pltpu.SMEM((slots, 1, n_row * rows), jnp.int32),
            pltpu.VMEM((4, rows, half * BS, BS), f32),
            pltpu.VMEM((3 * rows, slots, BS, BS), f32),
            pltpu.VMEM((3 * rows * slots + 1, BS, BS), BF),
            pltpu.VMEM((3 * rows * slots + 1, BS, BS), BF),
            pltpu.VMEM((2, BS, n_col * half * BS), BF),
            pltpu.VMEM((rows, half, BS, 2 * BS), f32),
            pltpu.VMEM((rows, half, BS, BS), f32),
            pltpu.VMEM((rows, half, BS, BS), f32),
            pltpu.SMEM((rows * n_col * half * slots,), jnp.int32),
            dma((2,)),
            dma((2, chunks)),
            dma((2,)),
            dma((rows,)),
            dma((2,)),
            dma((2, chunks)),
            dma((2,)),
            dma((2, chunks)),
            dma,
            dma((rows,)),
            dma,
            dma((chunks,)),
            dma((2,)),
        ],
        compiler_params=pltpu.CompilerParams(
            collective_id=0, has_side_effects=True, vmem_limit_bytes=56 * 2**20
        ),
        cost_estimate=pl.CostEstimate(
            flops=9 * 10**9, bytes_accessed=10**7, transcendentals=0
        ),
    )(
        jnp.transpose(p_pattern, (2, 1, 0)),
        jnp.transpose(s_pattern, (2, 1, 0)),
        p_blocks.reshape(rows, half * BS, BS),
        s_blocks,
    )


def solution(mesh):
    in_specs = (
        P("row", "col", "depth", None, None),
        P("row", "col", None, None, None),
        P("row", None, None),
        P(None, "col", None),
    )
    out_specs = P("row", "col", "depth", None, None)
    return jax.shard_map(
        per_device, mesh=mesh, in_specs=in_specs, out_specs=out_specs, check_vma=False
    )
```

```python
import functools

import jax
import jax.numpy as jnp
from jax import lax
from jax.experimental import pallas as pl
from jax.experimental.pallas import tpu as pltpu
from jax.sharding import PartitionSpec as P

BS = 128
W = 10
MESH = pl.DeviceIdType.MESH
BF = jnp.bfloat16


def split(x):
    hi = x.astype(BF)
    return hi, (x - hi.astype(jnp.float32)).astype(BF)


def kernel(
    sizes,
    p_pat_in,
    s_pat_in,
    p_in,
    s_in,
    out,
    p_pat,
    s_pat,
    p_land,
    s_land,
    s_hi,
    s_lo,
    lhs,
    sums,
    part,
    got,
    table,
    p_send,
    p_recv,
    f_send,
    f_recv,
    s_send,
    s_recv,
    x_send,
    x_recv,
    e_send,
    e_recv,
    own_p,
    own_s,
    pat_sem,
):
    n_row, n_col, rows, half = sizes
    slots = 2 * half
    total = n_row * rows
    window = 3 * rows
    zero_block = window * slots
    chunks = rows // 2
    r, z, d = lax.axis_index("row"), lax.axis_index("col"), lax.axis_index("depth")
    sib = 1 - d
    row_to = (lax.rem(r + 1, n_row), lax.rem(r + n_row - 1, n_row))
    col_to = (lax.rem(z + 1, n_col), lax.rem(z + n_col - 1, n_col))
    first_row = r * rows

    def p_direct(k, t, count=2):
        return pltpu.make_async_remote_copy(
            src_ref=p_in.at[pl.ds(2 * t, count)],
            dst_ref=p_land.at[1 + k, pl.ds(2 * t, count)],
            send_sem=p_send.at[k],
            recv_sem=p_recv.at[k, t],
            device_id={"col": col_to[k]},
            device_id_type=MESH,
        )

    def p_forward(k, t, count=1):
        lines = half * BS // 2
        at = (pl.ds(t, count), pl.ds(k * lines, lines))
        return pltpu.make_async_remote_copy(
            src_ref=p_land.at[1 + k, *at],
            dst_ref=p_land.at[3, *at],
            send_sem=f_send.at[k],
            recv_sem=f_recv.at[t],
            device_id={"col": col_to[k]},
            device_id_type=MESH,
        )

    def p_forwarded(t):
        return pltpu.make_async_remote_copy(
            src_ref=p_land.at[1, t],
            dst_ref=p_land.at[3, t],
            send_sem=f_send.at[0],
            recv_sem=f_recv.at[t],
            device_id={"col": col_to[0]},
            device_id_type=MESH,
        )

    def s_direct(k, u, count=1):
        at = d * chunks + u
        return pltpu.make_async_remote_copy(
            src_ref=s_in.at[pl.ds(at, count), 0],
            dst_ref=s_land.at[pl.ds(2 * k * rows + at, count)],
            send_sem=s_send.at[k],
            recv_sem=s_recv.at[k, u],
            device_id={"row": row_to[k]},
            device_id_type=MESH,
        )

    def s_cross(k, u, count=1):
        at = pl.ds(2 * k * rows + d * chunks + u, count)
        return pltpu.make_async_remote_copy(
            src_ref=s_land.at[at],
            dst_ref=s_land.at[at],
            send_sem=x_send.at[k],
            recv_sem=x_recv.at[k, u],
            device_id={"depth": sib},
            device_id_type=MESH,
        )

    def exchange(i, first=0, count=half, lines=1):
        at = (pl.ds(i, lines), pl.ds(first, count))
        return pltpu.make_async_remote_copy(
            src_ref=part.at[*at],
            dst_ref=got.at[*at],
            send_sem=e_send,
            recv_sem=e_recv.at[i],
            device_id={"depth": sib},
            device_id_type=MESH,
        )

    def load_s(u):
        at = pl.ds(2 * u, 2)
        return pltpu.make_async_copy(
            s_in.at[at, 0], s_land.at[pl.ds(rows + 2 * u, 2)], own_s.at[u]
        )

    def convert(at):
        for b in range(slots):
            hi, lo = split(s_land[at, b])
            s_hi[at * slots + b] = hi
            s_lo[at * slots + b] = lo

    def index_row(i):
        for q, shift in enumerate((0, n_col - 1, 1, 2)):
            group = lax.rem(z + shift, n_col)
            for a in range(half):
                col = p_pat[d * half + a, group, i]
                safe = jnp.maximum(col, 0)
                at = safe - first_row + W
                at = jnp.where(at < 0, at + total, at)
                at = jnp.where(at >= total, at - total, at)
                at = jnp.clip(at, 0, window - 1)
                have = [s_pat[b, 0, safe] for b in range(slots)]
                for c in range(slots):
                    target = p_pat[lax.rem(c + d * half, slots), z, i]
                    wanted = jnp.where(col >= 0, target, -1)
                    found = jnp.int32(zero_block)
                    for b in range(slots):
                        found = jnp.where(have[b] == wanted, at * slots + b, found)
                    found = jnp.where(wanted >= 0, found, zero_block)
                    table[(i * n_col * half + q * half + a) * slots + c] = found

    barrier = pltpu.get_barrier_semaphore()
    for k in range(2):
        pl.semaphore_signal(barrier, inc=1, device_id={"row": row_to[k]}, device_id_type=MESH)
        pl.semaphore_signal(barrier, inc=1, device_id={"col": col_to[k]}, device_id_type=MESH)
    pl.semaphore_signal(barrier, inc=1, device_id={"depth": sib}, device_id_type=MESH)
    pl.semaphore_wait(barrier, 5)

    for start in (p_direct, s_direct):

        @pl.loop(0, chunks)
        def _(u):
            for k in range(2):
                start(k, u).start()

    patterns = [
        pltpu.make_async_copy(p_pat_in, p_pat, pat_sem.at[0]),
        pltpu.make_async_copy(s_pat_in, s_pat, pat_sem.at[1]),
    ]
    for copy in patterns:
        copy.start()

    load_p = pltpu.make_async_copy(p_in, p_land.at[0], own_p)
    load_p.start()

    @pl.loop(0, chunks)
    def _(u):
        load_s(u).start()

    for copy in patterns:
        copy.wait()
    s_hi[zero_block] = jnp.zeros((BS, BS), BF)
    s_lo[zero_block] = jnp.zeros((BS, BS), BF)

    @pl.loop(0, chunks)
    def _(u):
        for t in range(2):
            index_row(2 * u + t)
        load_s(u).wait()
        for t in range(2):
            convert(rows + 2 * u + t)

    def pass_on(u):
        for k in range(2):
            p_direct(k, u).wait_recv()
        for t in range(2):
            for k in range(2):
                p_forward(k, 2 * u + t).start()

    @pl.loop(0, chunks)
    def _(u):
        for k in range(2):
            s_direct(k, u).wait_recv()
            s_cross(k, u).start()
        for k in range(2):
            convert(2 * k * rows + d * chunks + u)
        for k in range(2):
            s_cross(k, u).wait_recv()
            convert(2 * k * rows + sib * chunks + u)

        @pl.when(u < chunks - 1)
        def _():
            pass_on(u)

    inner = n_col * half

    def finish(i):
        exchange(i).wait_recv()
        for c in range(half):
            out[i, 0, c] = out[i, 0, c] + got[i, c]

    direct = 3 * half
    load_p.wait()

    def spread(i, first, last):
        for n in range(first, last):
            block = slice(n % half * BS, (n % half + 1) * BS)
            hi, lo = split(p_land[n // half, i, block])
            lhs[0, :, n * BS : (n + 1) * BS] = hi
            lhs[1, :, n * BS : (n + 1) * BS] = lo

    def multiply(i, tile, first, last, acc, picked=(0, 1)):
        terms = [
            (left, right, n)
            for left, right in ((0, s_hi), (1, s_hi), (0, s_lo))
            for n in range(first, last)
        ]
        for at in range(0, len(terms), 2):
            pair = terms[at : at + 2]
            wide = jnp.concatenate(
                [lhs[left, :, n * BS : (n + 1) * BS] for left, _, n in pair], axis=1
            )
            deep = jnp.concatenate(
                [
                    jnp.concatenate(
                        [
                            right[table[(i * inner + n) * slots + 2 * tile + c]]
                            for c in picked
                        ],
                        axis=1,
                    )
                    for _, right, n in pair
                ],
                axis=0,
            )
            term = jnp.dot(wide, deep, preferred_element_type=jnp.float32)
            acc = term if acc is None else acc + term
        return acc

    def begin(i):
        spread(i, 0, direct)
        for tile in range(slots // 2):
            sums[i, tile] = multiply(i, tile, 0, direct, None)

    def complete(i):
        p_forwarded(i).wait_recv()
        spread(i, direct, inner)
        for tile, picked in ((2, (0, 1)), (1, (1,)), (1, (0,)), (0, (0, 1))):
            start = picked[0] * BS
            width = len(picked) * BS
            before = sums[i, tile, :, start : start + width]
            acc = multiply(i, tile, direct, inner, before, picked)
            for at, c in enumerate(picked):
                slot = 2 * tile + c
                value = acc[:, at * BS : (at + 1) * BS]
                if slot < half:
                    out[i, 0, slot] = value
                else:
                    part[i, slot - half] = value
            if (tile, picked) == (2, (0, 1)):
                exchange(i, 1, 2).start()
            if (tile, picked) == (1, (1,)):
                exchange(i, 0, 1).start()

    @pl.loop(0, rows + 1)
    def _(j):
        @pl.when(j == 5)
        def _():
            pass_on(chunks - 1)

        @pl.when(j < rows)
        def _():
            begin(j)

        @pl.when(j == rows - 1)
        def _():
            for k in range(2):
                p_direct(k, 0, rows).wait_send()
                s_direct(k, 0, chunks).wait_send()
                s_cross(k, 0, chunks).wait_send()

        @pl.when(j > 0)
        def _():
            complete(j - 1)

        @pl.when(j > 1)
        def _():
            finish(j - 2)

    for k in range(2):
        p_forward(k, 0, rows).wait_send()
    finish(rows - 1)
    exchange(0, lines=rows).wait_send()


def per_device(p_blocks, s_blocks, p_pattern, s_pattern):
    rows, _, half = p_blocks.shape[:3]
    n_row, n_col = lax.axis_size("row"), lax.axis_size("col")
    slots = 2 * half
    f32 = jnp.float32
    dma = pltpu.SemaphoreType.DMA
    chunks = rows // 2
    return pl.pallas_call(
        functools.partial(kernel, (n_row, n_col, rows, half)),
        out_shape=pltpu.VMEM(p_blocks.shape, f32),
        in_specs=[pl.BlockSpec(memory_space=pl.ANY)] * 4,
        out_specs=pl.BlockSpec(memory_space=pltpu.VMEM),
        scratch_shapes=[
            pltpu.SMEM((slots, n_col, rows), jnp.int32),
            pltpu.SMEM((slots, 1, n_row * rows), jnp.int32),
            pltpu.VMEM((4, rows, half * BS, BS), f32),
            pltpu.VMEM((3 * rows, slots, BS, BS), f32),
            pltpu.VMEM((3 * rows * slots + 1, BS, BS), BF),
            pltpu.VMEM((3 * rows * slots + 1, BS, BS), BF),
            pltpu.VMEM((2, BS, n_col * half * BS), BF),
            pltpu.VMEM((rows, half, BS, 2 * BS), f32),
            pltpu.VMEM((rows, half, BS, BS), f32),
            pltpu.VMEM((rows, half, BS, BS), f32),
            pltpu.SMEM((rows * n_col * half * slots,), jnp.int32),
            dma((2,)),
            dma((2, chunks)),
            dma((2,)),
            dma((rows,)),
            dma((2,)),
            dma((2, chunks)),
            dma((2,)),
            dma((2, chunks)),
            dma,
            dma((rows,)),
            dma,
            dma((chunks,)),
            dma((2,)),
        ],
        compiler_params=pltpu.CompilerParams(
            collective_id=0, has_side_effects=True, vmem_limit_bytes=56 * 2**20
        ),
        cost_estimate=pl.CostEstimate(
            flops=9 * 10**9, bytes_accessed=10**7, transcendentals=0
        ),
    )(
        jnp.transpose(p_pattern, (2, 1, 0)),
        jnp.transpose(s_pattern, (2, 1, 0)),
        p_blocks.reshape(rows, half * BS, BS),
        s_blocks,
    )


def solution(mesh):
    in_specs = (
        P("row", "col", "depth", None, None),
        P("row", "col", None, None, None),
        P("row", None, None),
        P(None, "col", None),
    )
    out_specs = P("row", "col", "depth", None, None)
    return jax.shard_map(
        per_device, mesh=mesh, in_specs=in_specs, out_specs=out_specs, check_vma=False
    )
```

```python
import functools

import jax
import jax.numpy as jnp
from jax import lax
from jax.experimental import pallas as pl
from jax.experimental.pallas import tpu as pltpu
from jax.sharding import PartitionSpec as P

BS = 128
W = 10
MESH = pl.DeviceIdType.MESH
BF = jnp.bfloat16


def split(x):
    hi = x.astype(BF)
    return hi, (x - hi.astype(jnp.float32)).astype(BF)


def kernel(
    sizes,
    p_pat_in,
    s_pat_in,
    p_in,
    s_in,
    out,
    p_pat,
    s_pat,
    p_land,
    s_land,
    s_hi,
    s_lo,
    lhs,
    sums,
    part,
    got,
    table,
    p_send,
    p_recv,
    f_send,
    f_recv,
    s_send,
    s_recv,
    x_send,
    x_recv,
    e_send,
    e_recv,
    own_p,
    own_s,
    pat_sem,
):
    n_row, n_col, rows, half = sizes
    slots = 2 * half
    total = n_row * rows
    window = 3 * rows
    zero_block = window * slots
    chunks = rows // 2
    r, z, d = lax.axis_index("row"), lax.axis_index("col"), lax.axis_index("depth")
    sib = 1 - d
    row_to = (lax.rem(r + 1, n_row), lax.rem(r + n_row - 1, n_row))
    col_to = (lax.rem(z + 1, n_col), lax.rem(z + n_col - 1, n_col))
    first_row = r * rows

    def p_direct(k, t, count=2):
        return pltpu.make_async_remote_copy(
            src_ref=p_in.at[pl.ds(2 * t, count)],
            dst_ref=p_land.at[1 + k, pl.ds(2 * t, count)],
            send_sem=p_send.at[k],
            recv_sem=p_recv.at[k, t],
            device_id={"col": col_to[k]},
            device_id_type=MESH,
        )

    def p_forward(k, t, count=1):
        lines = half * BS // 2
        at = (pl.ds(t, count), pl.ds(k * lines, lines))
        return pltpu.make_async_remote_copy(
            src_ref=p_land.at[1 + k, *at],
            dst_ref=p_land.at[3, *at],
            send_sem=f_send.at[k],
            recv_sem=f_recv.at[t],
            device_id={"col": col_to[k]},
            device_id_type=MESH,
        )

    def p_forwarded(t):
        return pltpu.make_async_remote_copy(
            src_ref=p_land.at[1, t],
            dst_ref=p_land.at[3, t],
            send_sem=f_send.at[0],
            recv_sem=f_recv.at[t],
            device_id={"col": col_to[0]},
            device_id_type=MESH,
        )

    def s_direct(k, u, count=1):
        at = d * chunks + u
        return pltpu.make_async_remote_copy(
            src_ref=s_in.at[pl.ds(at, count), 0],
            dst_ref=s_land.at[pl.ds(2 * k * rows + at, count)],
            send_sem=s_send.at[k],
            recv_sem=s_recv.at[k, u],
            device_id={"row": row_to[k]},
            device_id_type=MESH,
        )

    def s_cross(k, u, count=1):
        at = pl.ds(2 * k * rows + d * chunks + u, count)
        return pltpu.make_async_remote_copy(
            src_ref=s_land.at[at],
            dst_ref=s_land.at[at],
            send_sem=x_send.at[k],
            recv_sem=x_recv.at[k, u],
            device_id={"depth": sib},
            device_id_type=MESH,
        )

    def exchange(i, first=0, count=half, lines=1):
        at = (pl.ds(i, lines), pl.ds(first, count))
        return pltpu.make_async_remote_copy(
            src_ref=part.at[*at],
            dst_ref=got.at[*at],
            send_sem=e_send,
            recv_sem=e_recv.at[i],
            device_id={"depth": sib},
            device_id_type=MESH,
        )

    def load_s(u):
        at = pl.ds(2 * u, 2)
        return pltpu.make_async_copy(
            s_in.at[at, 0], s_land.at[pl.ds(rows + 2 * u, 2)], own_s.at[u]
        )

    def convert(at):
        for b in range(slots):
            hi, lo = split(s_land[at, b])
            s_hi[at * slots + b] = hi
            s_lo[at * slots + b] = lo

    def index_row(i):
        for q, shift in enumerate((0, n_col - 1, 1, 2)):
            group = lax.rem(z + shift, n_col)
            for a in range(half):
                col = p_pat[d * half + a, group, i]
                safe = jnp.maximum(col, 0)
                at = safe - first_row + W
                at = jnp.where(at < 0, at + total, at)
                at = jnp.where(at >= total, at - total, at)
                at = jnp.clip(at, 0, window - 1)
                have = [s_pat[b, 0, safe] for b in range(slots)]
                for c in range(slots):
                    target = p_pat[lax.rem(c + d * half, slots), z, i]
                    wanted = jnp.where(col >= 0, target, -1)
                    found = jnp.int32(zero_block)
                    for b in range(slots):
                        found = jnp.where(have[b] == wanted, at * slots + b, found)
                    found = jnp.where(wanted >= 0, found, zero_block)
                    table[(i * n_col * half + q * half + a) * slots + c] = found

    barrier = pltpu.get_barrier_semaphore()
    for k in range(2):
        pl.semaphore_signal(barrier, inc=1, device_id={"row": row_to[k]}, device_id_type=MESH)
        pl.semaphore_signal(barrier, inc=1, device_id={"col": col_to[k]}, device_id_type=MESH)
    pl.semaphore_signal(barrier, inc=1, device_id={"depth": sib}, device_id_type=MESH)
    pl.semaphore_wait(barrier, 5)

    for start in (p_direct, s_direct):

        @pl.loop(0, chunks)
        def _(u):
            for k in range(2):
                start(k, u).start()

    patterns = [
        pltpu.make_async_copy(p_pat_in, p_pat, pat_sem.at[0]),
        pltpu.make_async_copy(s_pat_in, s_pat, pat_sem.at[1]),
    ]
    for copy in patterns:
        copy.start()

    load_p = pltpu.make_async_copy(p_in, p_land.at[0], own_p)
    load_p.start()

    @pl.loop(0, chunks)
    def _(u):
        load_s(u).start()

    for copy in patterns:
        copy.wait()
    s_hi[zero_block] = jnp.zeros((BS, BS), BF)
    s_lo[zero_block] = jnp.zeros((BS, BS), BF)

    @pl.loop(0, chunks)
    def _(u):
        for t in range(2):
            index_row(2 * u + t)
        load_s(u).wait()
        for t in range(2):
            convert(rows + 2 * u + t)

    def pass_on(u):
        for k in range(2):
            p_direct(k, u).wait_recv()
        for t in range(2):
            for k in range(2):
                p_forward(k, 2 * u + t).start()

    @pl.loop(0, chunks)
    def _(u):
        for k in range(2):
            s_direct(k, u).wait_recv()
            s_cross(k, u).start()
        for k in range(2):
            convert(2 * k * rows + d * chunks + u)
        for k in range(2):
            s_cross(k, u).wait_recv()
            convert(2 * k * rows + sib * chunks + u)

        @pl.when(u < chunks - 1)
        def _():
            pass_on(u)

    inner = n_col * half

    def finish(i):
        exchange(i).wait_recv()
        for c in range(half):
            out[i, 0, c] = out[i, 0, c] + got[i, c]

    direct = 3 * half
    load_p.wait()

    def spread(i, first, last):
        for n in range(first, last):
            block = slice(n % half * BS, (n % half + 1) * BS)
            hi, lo = split(p_land[n // half, i, block])
            lhs[0, :, n * BS : (n + 1) * BS] = hi
            lhs[1, :, n * BS : (n + 1) * BS] = lo

    def multiply(i, tile, first, last, acc):
        terms = [
            (left, right, n)
            for left, right in ((0, s_hi), (1, s_hi), (0, s_lo))
            for n in range(first, last)
        ]
        for at in range(0, len(terms), 2):
            pair = terms[at : at + 2]
            wide = jnp.concatenate(
                [lhs[left, :, n * BS : (n + 1) * BS] for left, _, n in pair], axis=1
            )
            deep = jnp.concatenate(
                [
                    jnp.concatenate(
                        [
                            right[table[(i * inner + n) * slots + 2 * tile + c]]
                            for c in range(2)
                        ],
                        axis=1,
                    )
                    for _, right, n in pair
                ],
                axis=0,
            )
            term = jnp.dot(wide, deep, preferred_element_type=jnp.float32)
            acc = term if acc is None else acc + term
        return acc

    def begin(i):
        spread(i, 0, direct)
        for tile in range(slots // 2):
            sums[i, tile] = multiply(i, tile, 0, direct, None)

    def complete(i):
        p_forwarded(i).wait_recv()
        spread(i, direct, inner)
        for tile in reversed(range(slots // 2)):
            acc = multiply(i, tile, direct, inner, sums[i, tile])
            for c in range(2):
                slot = 2 * tile + c
                value = acc[:, c * BS : (c + 1) * BS]
                if slot < half:
                    out[i, 0, slot] = value
                else:
                    part[i, slot - half] = value
            if tile == 1:
                exchange(i).start()

    @pl.loop(0, rows + 1)
    def _(j):
        @pl.when(j == 5)
        def _():
            pass_on(chunks - 1)

        @pl.when(j < rows)
        def _():
            begin(j)

        @pl.when(j == rows - 1)
        def _():
            for k in range(2):
                p_direct(k, 0, rows).wait_send()
                s_direct(k, 0, chunks).wait_send()
                s_cross(k, 0, chunks).wait_send()

        @pl.when(j > 0)
        def _():
            complete(j - 1)

        @pl.when(j > 1)
        def _():
            finish(j - 2)

    finish(rows - 1)
    for k in range(2):
        p_forward(k, 0, rows).wait_send()
    exchange(0, lines=rows).wait_send()


def per_device(p_blocks, s_blocks, p_pattern, s_pattern):
    rows, _, half = p_blocks.shape[:3]
    n_row, n_col = lax.axis_size("row"), lax.axis_size("col")
    slots = 2 * half
    f32 = jnp.float32
    dma = pltpu.SemaphoreType.DMA
    chunks = rows // 2
    return pl.pallas_call(
        functools.partial(kernel, (n_row, n_col, rows, half)),
        out_shape=pltpu.VMEM(p_blocks.shape, f32),
        in_specs=[pl.BlockSpec(memory_space=pl.ANY)] * 4,
        out_specs=pl.BlockSpec(memory_space=pltpu.VMEM),
        scratch_shapes=[
            pltpu.SMEM((slots, n_col, rows), jnp.int32),
            pltpu.SMEM((slots, 1, n_row * rows), jnp.int32),
            pltpu.VMEM((4, rows, half * BS, BS), f32),
            pltpu.VMEM((3 * rows, slots, BS, BS), f32),
            pltpu.VMEM((3 * rows * slots + 1, BS, BS), BF),
            pltpu.VMEM((3 * rows * slots + 1, BS, BS), BF),
            pltpu.VMEM((2, BS, n_col * half * BS), BF),
            pltpu.VMEM((rows, half, BS, 2 * BS), f32),
            pltpu.VMEM((rows, half, BS, BS), f32),
            pltpu.VMEM((rows, half, BS, BS), f32),
            pltpu.SMEM((rows * n_col * half * slots,), jnp.int32),
            dma((2,)),
            dma((2, chunks)),
            dma((2,)),
            dma((rows,)),
            dma((2,)),
            dma((2, chunks)),
            dma((2,)),
            dma((2, chunks)),
            dma,
            dma((rows,)),
            dma,
            dma((chunks,)),
            dma((2,)),
        ],
        compiler_params=pltpu.CompilerParams(
            collective_id=0, has_side_effects=True, vmem_limit_bytes=56 * 2**20
        ),
        cost_estimate=pl.CostEstimate(
            flops=9 * 10**9, bytes_accessed=10**7, transcendentals=0
        ),
    )(
        jnp.transpose(p_pattern, (2, 1, 0)),
        jnp.transpose(s_pattern, (2, 1, 0)),
        p_blocks.reshape(rows, half * BS, BS),
        s_blocks,
    )


def solution(mesh):
    in_specs = (
        P("row", "col", "depth", None, None),
        P("row", "col", None, None, None),
        P("row", None, None),
        P(None, "col", None),
    )
    out_specs = P("row", "col", "depth", None, None)
    return jax.shard_map(
        per_device, mesh=mesh, in_specs=in_specs, out_specs=out_specs, check_vma=False
    )
```
